128 devices in a mesh: dp: 8 (over y, core), expert: 16 (over x, z).
Axes of the slice: x: 4, y: 4, z: 4, core: 2. Of those that a mesh axis runs over, the one named last changes fastest.
Arguments:
- query_rows: bfloat16 [256, 6144], P(('dp', 'expert')), may hold values from -256 to 256
- key_cache: bfloat16 [256, 128, 1024], P(('dp', 'expert')), may hold values from -6 to 6
- value_cache: bfloat16 [256, 128, 1024], P(('dp', 'expert')), may hold values from -6 to 6
- residual: bfloat16 [256, 6144], P(('dp', 'expert')), may hold values from -36 to 36
- norm_gain: float32 [6144], replicated, may hold values from 0.1 to 1.9
- expert_ids: int32 [256, 4], P(('dp', 'expert')), may hold values from 0 to 15, all different within a row; in each aligned block of 32 rows (0 to 31, 32 to 63, ...) at most 16 rows name the same one
- route_weights: float32 [256, 4], P(('dp', 'expert')), may hold values from 0.1 to 0.6
- w_gate: bfloat16 [16, 6144, 5376], P('expert', None, 'dp'), may hold values from -0.078125 to 0.078125
- w_up: bfloat16 [16, 6144, 5376], P('expert', None, 'dp'), may hold values from -0.078125 to 0.078125
- w_down: bfloat16 [16, 5376, 6144], P('expert', 'dp'), may hold values from -0.078125 to 0.078125
Outputs:
- layer_out: bfloat16 [256, 6144], P(('dp', 'expert'))
The draws below stay inside these ranges and needn't reach their ends.
Inputs may be any that keep to these rules, and one draw needn't show every extreme that they name: `expert_ids`: each row names 4 different experts. In each aligned block of 32 rows (the rows of one index of dp) no expert is named by more than 16 rows, and in some of these blocks one expert is named by exactly 16.
All inputs are finite; a program needn't handle non-finite values.
Results may differ from the reference program's by a relative error of at most 0.006.
Values may be sent and summed in bfloat16 or wider, within the bound.
A program may use at most 128 MiB of HBM per device.

```python
import math
import jax
import jax.numpy as jnp
import numpy as np
from jax import lax

D = 6144
H = 48
KVH = 8
HD = 128
TOPK = 4
FF_WIN = 5376
ROW_DEV = 2
CTX = 128
EXPERTS = 16
ROWS = 256
M_GRP = 16
N_DP = 8
N_EXPERT = 16


def key_base(key):
    return jnp.clip(jax.random.normal(key, (ROWS, CTX, KVH * HD), jnp.float32), -6.0, 6.0)


def draw_key_cache(key, part):
    base_keys = key_base(key)
    return base_keys.astype(jnp.bfloat16)


def draw_query_rows(key, part):
    key = jax.random.fold_in(key, 5)
    jitter = jnp.clip(jax.random.normal(key, (ROWS, H * HD), jnp.float32), -6.0, 6.0)
    result = jitter
    return result.astype(jnp.bfloat16)


def draw_residual(key, part):
    key = jax.random.fold_in(key, 7)
    first_key, second_key, third_key = jax.random.split(key, 3)
    col_scale = jnp.exp(jax.random.uniform(second_key, (1, D), jnp.float32, math.log(0.3), math.log(3.0)))
    row_scale = jnp.exp(jax.random.uniform(first_key, (ROWS, 1), jnp.float32, math.log(0.3), math.log(3.0)))
    entries = jnp.clip(jax.random.normal(third_key, (ROWS, D), jnp.float32), -4.0, 4.0)
    return (row_scale * col_scale * entries).astype(jnp.bfloat16)


def levels(stream_key, shape, pieces, least, top_value):
    level, own = 1.0, jax.random.fold_in(stream_key, 6)
    for position, blocks in pieces:
        steps = jnp.exp(jax.random.uniform(jax.random.fold_in(own, position), (blocks,), jnp.float32, least / len(pieces), top_value / len(pieces)))
        level = level * jnp.repeat(steps, shape[position] // blocks).reshape([-1 if axis == position else 1 for axis in range(len(shape))])
    return level


def assign_block(key, own, number, rows, count, top, reach, slope):
    ranking = jax.random.permutation(key, count)
    packed, common = portions_of(count, rows * top, reach, slope, True), portions_of(count, rows * top, reach, slope, False)
    places = jnp.arange(count)

    def named(lengths, turn):
        used = int((lengths > 0).sum())
        fixed = max(1, used // 4)
        moved = fixed + (places - fixed + turn * (used - fixed)) % max(1, count - fixed)
        return jnp.zeros((count,), jnp.int32).at[ranking[jnp.where(places < fixed, places, moved)]].set(jnp.asarray(lengths, jnp.int32))

    lengths = jnp.where(number % 4 == 0, named(packed, number // 4), named(common, number - number // 4 - 1))
    mixed = jax.random.permutation(jax.random.fold_in(own, 3), count)
    giver, taker = mixed[0:count // 2 * 2:2], mixed[1:count // 2 * 2:2]
    margin = jnp.minimum(lengths[giver] - 1, reach - lengths[taker]) // 2
    margin = jnp.where((giver == ranking[0]) | (taker == ranking[0]) | (lengths[taker] == 0), 0, jnp.maximum(margin, 0))
    moved = jax.random.randint(jax.random.fold_in(own, 4), (count // 2,), 0, 1 << 20) % (margin + 1)
    lengths = lengths.at[giver].add(-moved).at[taker].add(moved)
    items = jnp.searchsorted(jnp.cumsum(lengths), jnp.arange(rows * top), side="right").astype(jnp.int32)
    table = items.reshape(top, rows).T
    table = table[jax.random.permutation(jax.random.fold_in(own, 1), rows)]
    turn = jax.random.randint(jax.random.fold_in(own, 2), (rows, 1), 0, top)
    return jnp.take_along_axis(table, (jnp.arange(top)[None, :] + turn) % top, axis=1)


def portions_of(count, total, bound, lean, full):
    weights = [(1 << 20) // math.isqrt(rank ** lean) + 1 for rank in range(1, count + 1)]
    largest = bound if full else min(bound, max(-(-total // count), total * weights[0] // sum(weights)))
    least = 1 if total - largest >= count - 1 else 0
    given, spare = [largest] + [least] * (count - 1), total - largest - least * (count - 1)
    while spare > 0:
        movable = [i for i in range(1, count) if given[i] < largest] or [i for i in range(1, count) if given[i] < bound]
        mass, remaining = sum([weights[i] for i in movable]), spare
        for i in movable:
            addition = min(bound - given[i], max(1, remaining * weights[i] // mass), spare)
            given[i] = given[i] + addition
            spare = spare - addition
    return np.array(given)


def scatter_about(rng, shape, spread, limit, pieces=(), kind=jnp.bfloat16):
    gain = levels(rng, shape, pieces, -0.22, 0.18) if pieces else 1.0
    values = jax.random.normal(rng, shape, jnp.float32) * spread * gain
    return jnp.minimum(jnp.maximum(values, -limit), limit).astype(kind)


def setup_inputs(seed: int = 0) -> dict:
    keys = jax.random.split(jax.random.key(seed), 11)
    query_rows = draw_query_rows(jax.random.fold_in(keys[10], 71), 0)
    key_cache = draw_key_cache(jax.random.fold_in(keys[10], 71), 0)
    value_cache = scatter_about(keys[2], (ROWS, CTX, KVH * HD), 1.0, 6.0, ((0, 128),))
    residual = draw_residual(jax.random.fold_in(keys[10], 71), 0)
    norm_gain = jnp.clip(1.0 + 0.18 * jax.random.normal(keys[4], (D,), jnp.float32), 0.1, 1.9)
    expert_ids_keys = jax.random.split(jax.random.fold_in(keys[5], 1), ROWS // (ROW_DEV * N_EXPERT))
    expert_ids_turns = jax.random.permutation(jax.random.fold_in(keys[5], 3), ROWS // (ROW_DEV * N_EXPERT))
    expert_ids = jax.vmap(lambda own, number: assign_block(jax.random.fold_in(keys[5], 2), own, number, ROW_DEV * N_EXPERT, EXPERTS, TOPK, M_GRP, 2))(expert_ids_keys, expert_ids_turns).reshape((ROWS, TOPK))
    route_weights = jnp.clip(0.1 + 0.5 * jax.random.uniform(keys[6], (ROWS, TOPK), jnp.float32) ** levels(keys[6], (ROWS, TOPK), ((0, 128),), -0.2, 0.2), 0.1, 0.6)
    w_gate = scatter_about(keys[7], (EXPERTS, D, FF_WIN), D ** -0.5, 0.078125, ((0, 16), (2, 8)))
    w_up = scatter_about(keys[8], (EXPERTS, D, FF_WIN), D ** -0.5, 0.078125, ((0, 16), (2, 8)))
    w_down = scatter_about(keys[9], (EXPERTS, FF_WIN, D), FF_WIN ** -0.5, 0.078125, ((0, 16), (1, 8)))
    return dict(query_rows=query_rows, key_cache=key_cache, value_cache=value_cache, residual=residual, norm_gain=norm_gain, expert_ids=expert_ids, route_weights=route_weights, w_gate=w_gate, w_up=w_up, w_down=w_down)


def attend(query_rows, key_cache, value_cache):
    row_count = query_rows.shape[0]
    per_group = H // KVH
    query_heads = query_rows.astype(jnp.float32).reshape(row_count, KVH, per_group, HD)
    key_heads = key_cache.astype(jnp.float32).reshape(row_count, CTX, KVH, HD)
    value_heads = value_cache.astype(jnp.float32).reshape(row_count, CTX, KVH, HD)
    attn_scores = jnp.einsum('rkgd,rtkd->rkgt', query_heads, key_heads) * HD ** (-0.5)
    row_max = lax.optimization_barrier(jnp.max(attn_scores, axis=-1, keepdims=True))
    lifted = jnp.exp(attn_scores - row_max)
    attn_probs = (lifted / lax.optimization_barrier(jnp.sum(lifted, axis=-1, keepdims=True))).astype(jnp.bfloat16)
    attn_probs = lax.optimization_barrier(attn_probs).astype(jnp.float32)
    attended = jnp.einsum('rkgt,rtkd->rkgd', attn_probs, value_heads)
    return attended.reshape(row_count, D)

def layer_norm(hstate, norm_gain):
    widened = hstate.astype(jnp.float32)
    row_mean = lax.optimization_barrier(jnp.mean(widened, axis=-1, keepdims=True))
    centered = widened - row_mean
    row_var = lax.optimization_barrier(jnp.mean(centered * centered, axis=-1, keepdims=True))
    return (centered * lax.rsqrt(row_var + 1e-05) * norm_gain).astype(jnp.bfloat16)

def reference(query_rows, key_cache, value_cache, residual, norm_gain, expert_ids, route_weights, w_gate, w_up, w_down):
    attended = attend(query_rows, key_cache, value_cache)
    hstate = (residual.astype(jnp.float32) + attended).astype(jnp.bfloat16)
    normed = layer_norm(hstate, norm_gain)
    capacity = N_DP * M_GRP
    slices = FF_WIN // N_DP
    row_order = jnp.arange(ROWS, dtype=jnp.int32)

    def one_expert(accumulated, expert):
        chosen = expert_ids == expert
        picked = jnp.any(chosen, axis=1)
        row_weight = lax.optimization_barrier(jnp.sum(jnp.where(chosen, route_weights, jnp.zeros_like(route_weights)), axis=1))
        row_index = jnp.argsort(jnp.where(picked, row_order, row_order + ROWS))[:capacity].astype(jnp.int32)
        is_valid = picked[row_index]
        taken = normed[row_index]
        gate_proj = jnp.dot(taken, w_gate[expert], preferred_element_type=jnp.float32)
        up_proj = jnp.dot(taken, w_up[expert], preferred_element_type=jnp.float32)
        expert_act = (jax.nn.silu(gate_proj) * up_proj).astype(jnp.bfloat16)
        expert_act = lax.optimization_barrier(expert_act).astype(jnp.float32)
        hidden_parts = jnp.einsum('cpf,pfd->pcd', expert_act.reshape(capacity, N_DP, slices), w_down[expert].astype(jnp.float32).reshape(N_DP, slices, D))
        hidden_parts = lax.optimization_barrier(hidden_parts.astype(jnp.bfloat16)).astype(jnp.float32)
        expert_out = lax.optimization_barrier(jnp.sum(hidden_parts, axis=0)).astype(jnp.bfloat16)
        expert_out = lax.optimization_barrier(expert_out).astype(jnp.float32)
        contrib = jnp.where(is_valid[:, None], row_weight[row_index][:, None] * expert_out, jnp.zeros_like(expert_out))
        return (accumulated.at[row_index].add(contrib), None)
    accumulated, _ = lax.scan(one_expert, jnp.zeros((ROWS, D), jnp.float32), jnp.arange(EXPERTS, dtype=jnp.int32))
    return (hstate.astype(jnp.float32) + accumulated).astype(jnp.bfloat16)
```

```python
import jax
import jax.numpy as jnp
from jax import lax
from jax.experimental import pallas as pl
from jax.experimental.pallas import tpu as pltpu
from jax.sharding import PartitionSpec as P

MESH = pl.DeviceIdType.MESH
D = 6144
H = 48
KVH = 8
HD = 128
PER = H // KVH
TOPK = 4
CTX = 128
NY, NX, NZ = 4, 4, 4
PLANE = NX * NZ
CAP = 16
FF = 672
NC = 3
HC = H // NC
CW = D // NC
BF = jnp.bfloat16
F32 = jnp.float32


def bytes_wait(ref, sem):
    pltpu.make_async_copy(ref, ref, sem).wait()


def across(a, b):
    return lax.dot_general(a, b, (((1,), (1,)), ((), ())), preferred_element_type=F32)


def kernel(
    ids_s,
    wts_s,
    q_ref,
    res_ref,
    gain_ref,
    key_hbm,
    val_hbm,
    gate_hbm,
    up_hbm,
    down_hbm,
    out_ref,
    key_v,
    val_v,
    gate_v,
    up_v,
    down_v,
    rows_q,
    rows_res,
    hst,
    mine,
    mine_ids,
    ids_in,
    x_in,
    flat,
    x_t,
    x_all,
    acc_g,
    acc_u,
    act,
    part,
    pair_in,
    summed,
    y_in,
    ret,
    r_in,
    sem_kv,
    sem_w,
    send_i,
    recv_i,
    send_a,
    recv_a,
    send_y,
    recv_y,
    send_p,
    recv_p,
    send_q,
    recv_q,
    send_z,
    recv_z,
    send_r,
    recv_r,
):
    p = lax.axis_index("dp")
    e = lax.axis_index("expert")
    y, core = p // 2, lax.rem(p, 2)
    x, z = e // NZ, lax.rem(e, NZ)
    offsets = [(i, j) for i in range(NX) for j in range(NZ)]

    def plane_dev(i, j):
        return (p, lax.rem(x + i + NX, NX) * NZ + lax.rem(z + j + NZ, NZ))

    def y_dev(dy):
        return (lax.rem(y + dy + NY, NY) * 2 + core, e)

    pair = (y * 2 + 1 - core, e)

    loads = []
    for r in range(2):
        for n, (src, dst) in enumerate(((key_hbm, key_v), (val_hbm, val_v))):
            cp = pltpu.make_async_copy(src.at[r], dst.at[r], sem_kv.at[2 * r + n])
            cp.start()
            loads.append(cp)
    w_loads = []
    for n, (src, dst) in enumerate(((gate_hbm, gate_v), (up_hbm, up_v), (down_hbm, down_v))):
        cp = pltpu.make_async_copy(src.at[0], dst, sem_w.at[n])
        cp.start()
        w_loads.append(cp)

    barrier = pltpu.get_barrier_semaphore()
    greet = [plane_dev(i, j) for i, j in offsets[1:]] + [y_dev(d) for d in range(1, NY)] + [pair]
    for dev in greet:
        pl.semaphore_signal(barrier, inc=1, device_id=dev, device_id_type=MESH)

    sub = lax.broadcasted_iota(jnp.int32, (8, 128), 0)
    lane = lax.broadcasted_iota(jnp.int32, (8, 128), 1)
    tile = jnp.zeros((8, 128), F32)
    for r in range(2):
        for k in range(TOPK):
            tile = jnp.where((sub == r) & (lane == ids_s[r, k]), 1.0, tile)
    mine_ids[...] = tile

    qf = q_ref[...].astype(F32)
    rf = res_ref[...].astype(F32)
    for h in range(H):
        rows_q[pl.ds(h, 2, stride=H), :] = qf[:, h * HD : (h + 1) * HD]
        rows_res[pl.ds(h, 2, stride=H), :] = rf[:, h * HD : (h + 1) * HD]
    head = lax.broadcasted_iota(jnp.int32, (H, HD), 0)
    masks = [(head >= PER * g) & (head < PER * (g + 1)) for g in range(KVH)]
    gain = gain_ref[...]
    for r in range(2):
        q = rows_q[pl.ds(r * H, H), :]
        q_wide = jnp.concatenate([jnp.where(m, q, 0.0) for m in masks], axis=1).astype(BF)
        loads[2 * r].wait()
        scores = lax.dot_general(
            q_wide, key_v[r], (((1,), (1,)), ((), ())), preferred_element_type=F32
        ) * HD ** (-0.5)
        lifted = jnp.exp(scores - jnp.max(scores, axis=1, keepdims=True))
        probs = (lifted / jnp.sum(lifted, axis=1, keepdims=True)).astype(BF)
        loads[2 * r + 1].wait()
        wide = jnp.dot(probs, val_v[r], preferred_element_type=F32)
        attended = jnp.zeros((H, HD), F32)
        for g in range(KVH):
            attended = jnp.where(masks[g], wide[:, g * HD : (g + 1) * HD], attended)
        hstate = (rows_res[pl.ds(r * H, H), :] + attended).astype(BF).astype(F32)
        hst[r] = hstate
        mean = jnp.sum(hstate) * (1.0 / D)
        centered = hstate - mean
        var = jnp.sum(centered * centered) * (1.0 / D)
        normed = (centered * lax.rsqrt(var + 1e-05) * gain).astype(BF)
        mine[r] = normed
        x_in[0, r] = normed

    pl.semaphore_wait(barrier, len(greet))

    for n, (i, j) in enumerate(offsets):
        if n:
            pltpu.make_async_remote_copy(
                src_ref=mine_ids, dst_ref=ids_in.at[n], send_sem=send_i.at[0],
                recv_sem=recv_i.at[0], device_id=plane_dev(i, j), device_id_type=MESH,
            ).start()
    for c in range(NC):
        for n, (i, j) in enumerate(offsets):
            if n:
                pltpu.make_async_remote_copy(
                    src_ref=mine.at[:, pl.ds(c * HC, HC)],
                    dst_ref=x_in.at[n, :, pl.ds(c * HC, HC)],
                    send_sem=send_a.at[c], recv_sem=recv_a.at[c],
                    device_id=plane_dev(i, j), device_id_type=MESH,
                ).start()
    ids_in[0] = mine_ids[...]
    bytes_wait(ids_in.at[pl.ds(1, PLANE - 1)], recv_i.at[0])

    table = ids_in[...].reshape(PLANE * 8, 128)
    rowi = lax.broadcasted_iota(jnp.int32, (2 * PLANE, PLANE * 8), 0)
    coli = lax.broadcasted_iota(jnp.int32, (2 * PLANE, PLANE * 8), 1)
    squeeze = jnp.where(coli == 4 * rowi - 3 * (rowi & 1), 1.0, 0.0)
    named = jnp.dot(squeeze, table, preferred_element_type=F32)
    mine_lane = lax.broadcasted_iota(jnp.int32, (2 * PLANE, 128), 1)
    picked_c = jnp.sum(jnp.where(mine_lane == e, named, 0.0), axis=1, keepdims=True)
    picked_b = jnp.broadcast_to(picked_c, (2 * PLANE, 128))
    ri = lax.broadcasted_iota(jnp.int32, (2 * PLANE, 2 * PLANE), 0)
    ci = lax.broadcasted_iota(jnp.int32, (2 * PLANE, 2 * PLANE), 1)
    below = jnp.where(ci < ri, 1.0, 0.0)
    rank_b = jnp.dot(below, picked_b, preferred_element_type=F32)
    spread_f = jnp.where(
        (rank_b == mine_lane.astype(F32)) & (picked_b > 0.5), 1.0, 0.0
    )
    spread = spread_f[:, :CAP].astype(BF)
    ident = jnp.where(ri == ci, 1.0, 0.0)
    pick = lax.dot_general(
        spread_f, ident, (((0,), (0,)), ((), ())), preferred_element_type=F32
    )[:CAP, :].astype(BF)

    def forward(c, dy):
        cp = pltpu.make_async_remote_copy(
            src_ref=x_all.at[c, dy], dst_ref=x_all.at[c, NY + dy], send_sem=send_p.at[c, dy],
            recv_sem=recv_p.at[c, dy], device_id=pair, device_id_type=MESH,
        )
        cp.start()
        return cp

    pair_copies = []
    for c in range(NC):
        bytes_wait(x_in.at[pl.ds(1, PLANE - 1), :, pl.ds(c * HC, HC)], recv_a.at[c])
        flat[...] = (
            x_in[:, :, c * HC : (c + 1) * HC, :].astype(F32).reshape(2 * PLANE * HC, HD)
        )
        for s in range(HC):
            x_t[:, s * HD : (s + 1) * HD] = flat[pl.ds(s, 2 * PLANE, stride=HC), :].astype(BF)
        x_all[c, 0] = jnp.dot(pick, x_t[...], preferred_element_type=F32).astype(BF)
        for dy in range(1, NY):
            pltpu.make_async_remote_copy(
                src_ref=x_all.at[c, 0], dst_ref=x_all.at[c, dy], send_sem=send_y.at[c],
                recv_sem=recv_y.at[c, dy], device_id=y_dev(dy), device_id_type=MESH,
            ).start()
        pair_copies.append(forward(c, 0))

    for c in range(NC):
        for dy in range(1, NY):
            bytes_wait(x_all.at[c, dy], recv_y.at[c, dy])
            pair_copies.append(forward(c, dy))
        for dy in range(NY):
            bytes_wait(x_all.at[c, NY + dy], recv_p.at[c, dy])
        if c == 0:
            w_loads[0].wait()
            w_loads[1].wait()
        block = x_all[c].reshape(2 * NY * CAP, CW)
        gate = across(gate_v[:, c * CW : (c + 1) * CW], block)
        up = across(up_v[:, c * CW : (c + 1) * CW], block)
        if c < NC - 1:
            acc_g[...] = gate if c == 0 else acc_g[...] + gate
            acc_u[...] = up if c == 0 else acc_u[...] + up
        else:
            gate = acc_g[...] + gate
            up = acc_u[...] + up
            act[...] = jnp.transpose(gate / (1.0 + jnp.exp(-gate)) * up).astype(BF)

    w_loads[2].wait()

    def down(n):
        out = jnp.dot(
            act[...], down_v[:, n * CW : (n + 1) * CW], preferred_element_type=F32
        ).astype(BF)
        part[n] = out.reshape(2 * NY, CAP, CW)
        pltpu.make_async_remote_copy(
            src_ref=part.at[n, pl.ds(NY, NY)], dst_ref=pair_in.at[n], send_sem=send_q.at[n],
            recv_sem=recv_q.at[n], device_id=pair, device_id_type=MESH,
        ).start()

    def pair_sum(n):
        bytes_wait(pair_in.at[n], recv_q.at[n])
        summed[n] = (part[n, :NY].astype(F32) + pair_in[n].astype(F32)).astype(BF)
        for dy in range(1, NY):
            pltpu.make_async_remote_copy(
                src_ref=summed.at[n, dy], dst_ref=y_in.at[n, dy - 1], send_sem=send_z.at[n],
                recv_sem=recv_z.at[n], device_id=y_dev(-dy), device_id_type=MESH,
            ).start()

    for n in range(NC):
        down(n)
        if n:
            pair_sum(n - 1)
    pair_sum(NC - 1)

    for n in range(NC):
        bytes_wait(y_in.at[n], recv_z.at[n])
        total = summed[n, 0].astype(F32)
        for dy in range(NY - 1):
            total = total + y_in[n, dy].astype(F32)
        back = jnp.dot(spread, total.astype(BF), preferred_element_type=F32)
        for s in range(HC):
            flat[pl.ds(s, 2 * PLANE, stride=HC), :] = back[:, s * HD : (s + 1) * HD]
        ret[n] = flat[...].astype(BF).reshape(PLANE, 2, HC, HD)
        for m, (i, j) in enumerate(offsets):
            if m:
                pltpu.make_async_remote_copy(
                    src_ref=ret.at[n, m], dst_ref=r_in.at[n, m], send_sem=send_r.at[n],
                    recv_sem=recv_r.at[n], device_id=plane_dev(-i, -j), device_id_type=MESH,
                ).start()

    weights = []
    for r in range(2):
        row = []
        for i, j in offsets:
            expert = plane_dev(i, j)[1]
            w = jnp.float32(0.0)
            for k in range(TOPK):
                w = w + jnp.where(ids_s[r, k] == expert, wts_s[r, k], 0.0)
            row.append(w)
        weights.append(row)
    for n in range(NC):
        bytes_wait(r_in.at[n, pl.ds(1, PLANE - 1)], recv_r.at[n])
        for r in range(2):
            total = hst[r, n * HC : (n + 1) * HC, :]
            for m in range(PLANE):
                got = ret[n, 0, r] if m == 0 else r_in[n, m, r]
                total = total + weights[r][m] * got.astype(F32)
            out_ref[r, n * HC : (n + 1) * HC, :] = total.astype(BF)

    bytes_wait(ids_in.at[pl.ds(1, PLANE - 1)], send_i.at[0])
    for c in range(NC):
        bytes_wait(x_in.at[pl.ds(1, PLANE - 1), :, pl.ds(c * HC, HC)], send_a.at[c])
        bytes_wait(x_all.at[c, pl.ds(1, NY - 1)], send_y.at[c])
        bytes_wait(pair_in.at[c], send_q.at[c])
        bytes_wait(y_in.at[c], send_z.at[c])
        bytes_wait(r_in.at[c, pl.ds(1, PLANE - 1)], send_r.at[c])
    for cp in pair_copies:
        cp.wait_send()


def body(q, key_cache, value_cache, residual, norm_gain, ids, wts, w_gate, w_up, w_down):
    vmem = pl.BlockSpec(memory_space=pltpu.VMEM)
    smem = pl.BlockSpec(memory_space=pltpu.SMEM)
    hbm = pl.BlockSpec(memory_space=pl.ANY)
    dma = pltpu.SemaphoreType.DMA
    out = pl.pallas_call(
        kernel,
        out_shape=jax.ShapeDtypeStruct((2, H, HD), BF),
        in_specs=[smem, smem, vmem, vmem, vmem] + [hbm] * 5,
        out_specs=vmem,
        scratch_shapes=[
            pltpu.VMEM((2, CTX, KVH * HD), BF),
            pltpu.VMEM((2, CTX, KVH * HD), BF),
            pltpu.VMEM((FF, D), BF),
            pltpu.VMEM((FF, D), BF),
            pltpu.VMEM((FF, D), BF),
            pltpu.VMEM((2 * H, HD), F32),
            pltpu.VMEM((2 * H, HD), F32),
            pltpu.VMEM((2, H, HD), F32),
            pltpu.VMEM((2, H, HD), BF),
            pltpu.VMEM((8, 128), F32),
            pltpu.VMEM((PLANE, 8, 128), F32),
            pltpu.VMEM((PLANE, 2, H, HD), BF),
            pltpu.VMEM((2 * PLANE * HC, HD), F32),
            pltpu.VMEM((2 * PLANE, CW), BF),
            pltpu.VMEM((NC, 2 * NY, CAP, CW), BF),
            pltpu.VMEM((FF, 2 * NY * CAP), F32),
            pltpu.VMEM((FF, 2 * NY * CAP), F32),
            pltpu.VMEM((2 * NY * CAP, FF), BF),
            pltpu.VMEM((NC, 2 * NY, CAP, CW), BF),
            pltpu.VMEM((NC, NY, CAP, CW), BF),
            pltpu.VMEM((NC, NY, CAP, CW), BF),
            pltpu.VMEM((NC, NY - 1, CAP, CW), BF),
            pltpu.VMEM((NC, PLANE, 2, HC, HD), BF),
            pltpu.VMEM((NC, PLANE, 2, HC, HD), BF),
            dma((4,)),
            dma((3,)),
            dma((1,)),
            dma((1,)),
            dma((NC,)),
            dma((NC,)),
            dma((NC,)),
            dma((NC, NY)),
            dma((NC, NY)),
            dma((NC, NY)),
            dma((NC,)),
            dma((NC,)),
            dma((NC,)),
            dma((NC,)),
            dma((NC,)),
            dma((NC,)),
        ],
        compiler_params=pltpu.CompilerParams(
            collective_id=0, has_side_effects=True, vmem_limit_bytes=56 * 1024 * 1024
        ),
        cost_estimate=pl.CostEstimate(
            flops=6 * 128 * D * FF, bytes_accessed=3 * 2 * D * FF, transcendentals=128 * FF
        ),
        name="decode_layer",
    )(
        ids,
        wts,
        q,
        residual,
        norm_gain.reshape(H, HD),
        key_cache,
        value_cache,
        jnp.swapaxes(w_gate, 1, 2),
        jnp.swapaxes(w_up, 1, 2),
        w_down,
    )
    return out.reshape(2, D)


def solution(mesh):
    return jax.shard_map(
        body,
        mesh=mesh,
        in_specs=(
            P(("dp", "expert"), None),
            P(("dp", "expert"), None, None),
            P(("dp", "expert"), None, None),
            P(("dp", "expert"), None),
            P(),
            P(("dp", "expert"), None),
            P(("dp", "expert"), None),
            P("expert", None, "dp"),
            P("expert", None, "dp"),
            P("expert", "dp", None),
        ),
        out_specs=P(("dp", "expert"), None),
        check_vma=False,
    )
```

```python
import jax
import jax.numpy as jnp
from jax import lax
from jax.experimental import pallas as pl
from jax.experimental.pallas import tpu as pltpu
from jax.sharding import PartitionSpec as P

MESH = pl.DeviceIdType.MESH
D = 6144
H = 48
KVH = 8
HD = 128
PER = H // KVH
TOPK = 4
CTX = 128
NY, NX, NZ = 4, 4, 4
PLANE = NX * NZ
CAP = 16
FF = 672
NC = 6
LAG = 3
EARLY = 4
FIRST = 4
HC = H // NC
CW = D // NC
BF = jnp.bfloat16
F32 = jnp.float32


def bytes_wait(ref, sem):
    pltpu.make_async_copy(ref, ref, sem).wait()


def across(a, b):
    return lax.dot_general(a, b, (((1,), (1,)), ((), ())), preferred_element_type=F32)


def total_of(a):
    return jnp.sum(jnp.sum(a, axis=0, keepdims=True), axis=1, keepdims=True)


def kernel(
    ids_hbm,
    wts_hbm,
    q_hbm,
    res_hbm,
    gain_hbm,
    key_hbm,
    val_hbm,
    gate_hbm,
    up_hbm,
    down_hbm,
    out_ref,
    ids_s,
    wts_s,
    q_ref,
    res_ref,
    gain_ref,
    key_v,
    val_v,
    gate_v,
    up_v,
    down_v,
    gate_t,
    up_t,
    rows_q,
    rows_res,
    hst,
    mine,
    mine_ids,
    ids_in,
    x_in,
    flat,
    x_t,
    x_all,
    acc_g,
    acc_u,
    act,
    part,
    pair_in,
    summed,
    y_in,
    ret,
    r_in,
    sem_in,
    sem_kv,
    sem_w,
    send_i,
    recv_i,
    send_a,
    recv_a,
    send_y,
    recv_y,
    send_p,
    recv_p,
    send_q,
    recv_q,
    send_z,
    recv_z,
    send_r,
    recv_r,
):
    p = lax.axis_index("dp")
    e = lax.axis_index("expert")
    y, core = p // 2, lax.rem(p, 2)
    x, z = e // NZ, lax.rem(e, NZ)
    offsets = [(i, j) for i in range(NX) for j in range(NZ)]

    def plane_dev(i, j):
        return (p, lax.rem(x + i + NX, NX) * NZ + lax.rem(z + j + NZ, NZ))

    def y_dev(dy):
        return (lax.rem(y + dy + NY, NY) * 2 + core, e)

    pair = (y * 2 + 1 - core, e)

    smalls = []
    for n, (src, dst) in enumerate(
        ((q_hbm, q_ref), (res_hbm, res_ref), (ids_hbm, ids_s), (wts_hbm, wts_s), (gain_hbm, gain_ref))
    ):
        cp = pltpu.make_async_copy(src, dst, sem_in.at[n])
        cp.start()
        smalls.append(cp)
    loads = []
    for r in range(2):
        for n, (src, dst) in enumerate(((key_hbm, key_v), (val_hbm, val_v))):
            cp = pltpu.make_async_copy(src.at[r], dst.at[r], sem_kv.at[2 * r + n])
            cp.start()
            loads.append(cp)

    barrier = pltpu.get_barrier_semaphore()
    greet = [plane_dev(i, j) for i, j in offsets[1:]] + [y_dev(d) for d in range(1, NY)] + [pair]
    for dev in greet:
        pl.semaphore_signal(barrier, inc=1, device_id=dev, device_id_type=MESH)

    smalls[0].wait()
    qf = q_ref[...].astype(F32)
    for h in range(H):
        rows_q[pl.ds(h, 2, stride=H), :] = qf[:, h * HD : (h + 1) * HD]
    head = lax.broadcasted_iota(jnp.int32, (H, HD), 0)
    masks = [(head >= PER * g) & (head < PER * (g + 1)) for g in range(KVH)]
    q_wide = []
    for r in range(2):
        q = rows_q[pl.ds(r * H, H), :]
        q_wide.append(
            jnp.concatenate([jnp.where(m, q, 0.0) for m in masks], axis=1).astype(BF)
        )
    smalls[1].wait()
    rf = res_ref[...].astype(F32)
    for h in range(H):
        rows_res[pl.ds(h, 2, stride=H), :] = rf[:, h * HD : (h + 1) * HD]
    for cp in smalls[2:]:
        cp.wait()

    lane = lax.broadcasted_iota(jnp.int32, (1, 128), 1)
    tile = jnp.zeros((1, 128), F32)
    for r in range(2):
        for k in range(TOPK):
            tile = jnp.where(lane == ids_s[r, k] + r * PLANE, 1.0, tile)
    mine_ids[...] = tile

    for cp in loads:
        cp.wait()
    w_loads = [
        pltpu.make_async_copy(
            src.at[0, :, pl.ds(c * CW, CW)], dst.at[:, pl.ds(c * CW, CW)], sem_w.at[2 * c + n]
        )
        for c in range(NC)
        for n, (src, dst) in enumerate(((gate_hbm, gate_v), (up_hbm, up_v)))
    ]
    w_loads.append(pltpu.make_async_copy(down_hbm.at[0], down_v, sem_w.at[2 * NC]))
    for cp in w_loads[: 2 * FIRST]:
        cp.start()

    def turn(c):
        for n, (src, dst) in enumerate(((gate_v, gate_t), (up_v, up_t))):
            w_loads[2 * c + n].wait()
            dst[c * CW : (c + 1) * CW, :] = jnp.transpose(src[:, c * CW : (c + 1) * CW])

    scores = jnp.concatenate([across(q_wide[r], key_v[r]) for r in range(2)], axis=0) * HD ** (-0.5)
    lifted = jnp.exp(scores - jnp.max(scores, axis=1, keepdims=True))
    probs = (lifted / jnp.sum(lifted, axis=1, keepdims=True)).astype(BF)
    gain = gain_ref[...]
    normed = []
    for r in range(2):
        wide = jnp.dot(probs[r * H : (r + 1) * H], val_v[r], preferred_element_type=F32)
        attended = jnp.zeros((H, HD), F32)
        for g in range(KVH):
            attended = jnp.where(masks[g], wide[:, g * HD : (g + 1) * HD], attended)
        hstate = (rows_res[pl.ds(r * H, H), :] + attended).astype(BF).astype(F32)
        hst[r] = hstate
        mean = total_of(hstate) * (1.0 / D)
        centered = hstate - mean
        var = total_of(centered * centered) * (1.0 / D)
        normed.append(centered * lax.rsqrt(var + 1e-05) * gain)
    for c in range(NC):
        block = jnp.concatenate([v[c * HC : (c + 1) * HC, :] for v in normed], axis=0).astype(BF)
        mine[c] = block
        x_in[c, 0] = block

    pl.semaphore_wait(barrier, len(greet))

    for n, (i, j) in enumerate(offsets):
        if n:
            pltpu.make_async_remote_copy(
                src_ref=mine_ids, dst_ref=ids_in.at[n], send_sem=send_i.at[0],
                recv_sem=recv_i.at[0], device_id=plane_dev(i, j), device_id_type=MESH,
            ).start()
    for c in range(NC):
        for n, (i, j) in enumerate(offsets):
            if n:
                pltpu.make_async_remote_copy(
                    src_ref=mine.at[c], dst_ref=x_in.at[c, n],
                    send_sem=send_a.at[c], recv_sem=recv_a.at[c],
                    device_id=plane_dev(i, j), device_id_type=MESH,
                ).start()
    for cp in w_loads[2 * FIRST :]:
        cp.start()
    for c in range(EARLY):
        turn(c)
    ids_in[0] = mine_ids[...]
    bytes_wait(ids_in.at[pl.ds(1, PLANE - 1)], recv_i.at[0])

    table = jnp.concatenate([ids_in[n] for n in range(PLANE)], axis=0)
    rowi = lax.broadcasted_iota(jnp.int32, (2 * PLANE, PLANE), 0)
    coli = lax.broadcasted_iota(jnp.int32, (2 * PLANE, PLANE), 1)
    twice = jnp.where(2 * coli == rowi - (rowi & 1), 1.0, 0.0)
    named = jnp.dot(twice, table, preferred_element_type=F32)
    mine_row = lax.broadcasted_iota(jnp.int32, (2 * PLANE, 128), 0)
    mine_lane = lax.broadcasted_iota(jnp.int32, (2 * PLANE, 128), 1)
    picked_c = jnp.sum(
        jnp.where(mine_lane == e + PLANE * (mine_row & 1), named, 0.0), axis=1, keepdims=True
    )
    picked_b = jnp.broadcast_to(picked_c, (2 * PLANE, 128))
    ri = lax.broadcasted_iota(jnp.int32, (2 * PLANE, 2 * PLANE), 0)
    ci = lax.broadcasted_iota(jnp.int32, (2 * PLANE, 2 * PLANE), 1)
    below = jnp.where(ci < ri, 1.0, 0.0)
    rank_b = jnp.dot(below, picked_b, preferred_element_type=F32)
    spread_f = jnp.where(
        (rank_b == mine_lane.astype(F32)) & (picked_b > 0.5), 1.0, 0.0
    )
    spread = spread_f[:, :CAP].astype(BF)
    ident = jnp.where(ri == ci, 1.0, 0.0)
    pick = lax.dot_general(
        spread_f, ident, (((0,), (0,)), ((), ())), preferred_element_type=F32
    )[:CAP, :].astype(BF)

    def forward(c, dy):
        cp = pltpu.make_async_remote_copy(
            src_ref=x_all.at[c, dy], dst_ref=x_all.at[c, NY + dy], send_sem=send_p.at[c, dy],
            recv_sem=recv_p.at[c, dy], device_id=pair, device_id_type=MESH,
        )
        cp.start()
        return cp

    pair_copies = []
    for c in range(NC):
        bytes_wait(x_in.at[c, pl.ds(1, PLANE - 1)], recv_a.at[c])
        flat[...] = x_in[c].astype(F32).reshape(2 * PLANE * HC, HD)
        for s in range(HC):
            x_t[:, s * HD : (s + 1) * HD] = flat[pl.ds(s, 2 * PLANE, stride=HC), :].astype(BF)
        x_all[c, 0] = jnp.dot(pick, x_t[...], preferred_element_type=F32).astype(BF)
        for dy in range(1, NY):
            pltpu.make_async_remote_copy(
                src_ref=x_all.at[c, 0], dst_ref=x_all.at[c, dy], send_sem=send_y.at[c],
                recv_sem=recv_y.at[c, dy], device_id=y_dev(dy), device_id_type=MESH,
            ).start()
        pair_copies.append(forward(c, 0))
        if c % 2 == 1 and EARLY + c // 2 < NC:
            turn(EARLY + c // 2)

    def forward_all(c):
        for dy in range(1, NY):
            bytes_wait(x_all.at[c, dy], recv_y.at[c, dy])
            pair_copies.append(forward(c, dy))

    def multiply(c):
        for dy in range(NY):
            bytes_wait(x_all.at[c, NY + dy], recv_p.at[c, dy])
        block = x_all[c].reshape(2 * NY * CAP, CW)
        gate = jnp.dot(block, gate_t[c * CW : (c + 1) * CW, :], preferred_element_type=F32)
        up = jnp.dot(block, up_t[c * CW : (c + 1) * CW, :], preferred_element_type=F32)
        if c < NC - 1:
            acc_g[...] = gate if c == 0 else acc_g[...] + gate
            acc_u[...] = up if c == 0 else acc_u[...] + up
        else:
            gate = acc_g[...] + gate
            up = acc_u[...] + up
            act[...] = (gate / (1.0 + jnp.exp(-gate)) * up).astype(BF)

    forward_all(0)
    for c in range(NC):
        if c < NC - 1:
            forward_all(c + 1)
        multiply(c)

    w_loads[2 * NC].wait()

    def down(n):
        out = jnp.dot(
            act[...], down_v[:, n * CW : (n + 1) * CW], preferred_element_type=F32
        ).astype(BF)
        part[n] = out.reshape(2 * NY, CAP, CW)
        pltpu.make_async_remote_copy(
            src_ref=part.at[n, pl.ds(NY, NY)], dst_ref=pair_in.at[n], send_sem=send_q.at[n],
            recv_sem=recv_q.at[n], device_id=pair, device_id_type=MESH,
        ).start()

    def pair_sum(n):
        bytes_wait(pair_in.at[n], recv_q.at[n])
        summed[n] = (part[n, :NY].astype(F32) + pair_in[n].astype(F32)).astype(BF)
        for dy in range(1, NY):
            pltpu.make_async_remote_copy(
                src_ref=summed.at[n, dy], dst_ref=y_in.at[n, dy - 1], send_sem=send_z.at[n],
                recv_sem=recv_z.at[n], device_id=y_dev(-dy), device_id_type=MESH,
            ).start()

    for n in range(NC):
        down(n)
        if n >= LAG:
            pair_sum(n - LAG)
    for n in range(NC - LAG, NC):
        pair_sum(n)

    for n in range(NC):
        bytes_wait(y_in.at[n], recv_z.at[n])
        total = summed[n, 0].astype(F32)
        for dy in range(NY - 1):
            total = total + y_in[n, dy].astype(F32)
        back = jnp.dot(spread, total.astype(BF), preferred_element_type=F32)
        for s in range(HC):
            flat[pl.ds(s, 2 * PLANE, stride=HC), :] = back[:, s * HD : (s + 1) * HD]
        ret[n] = flat[...].astype(BF).reshape(PLANE, 2 * HC, HD)
        for m, (i, j) in enumerate(offsets):
            if m:
                pltpu.make_async_remote_copy(
                    src_ref=ret.at[n, m], dst_ref=r_in.at[n, m], send_sem=send_r.at[n],
                    recv_sem=recv_r.at[n], device_id=plane_dev(-i, -j), device_id_type=MESH,
                ).start()

    weights = []
    for r in range(2):
        row = []
        for i, j in offsets:
            expert = plane_dev(i, j)[1]
            w = jnp.float32(0.0)
            for k in range(TOPK):
                w = w + jnp.where(ids_s[r, k] == expert, wts_s[r, k], 0.0)
            row.append(w)
        weights.append(row)
    for n in range(NC):
        bytes_wait(r_in.at[n, pl.ds(1, PLANE - 1)], recv_r.at[n])
        replies = [ret[n, 0].astype(F32)] + [r_in[n, m].astype(F32) for m in range(1, PLANE)]
        for r in range(2):
            total = hst[r, n * HC : (n + 1) * HC, :]
            for m in range(PLANE):
                got = replies[m][r * HC : (r + 1) * HC, :]
                total = total + weights[r][m] * got
            rows_q[pl.ds(r * H + n * HC, HC), :] = total
    for h in range(H):
        out_ref[:, h * HD : (h + 1) * HD] = rows_q[pl.ds(h, 2, stride=H), :].astype(BF)

    bytes_wait(ids_in.at[pl.ds(1, PLANE - 1)], send_i.at[0])
    for c in range(NC):
        bytes_wait(x_in.at[c, pl.ds(1, PLANE - 1)], send_a.at[c])
        bytes_wait(x_all.at[c, pl.ds(1, NY - 1)], send_y.at[c])
        bytes_wait(pair_in.at[c], send_q.at[c])
        bytes_wait(y_in.at[c], send_z.at[c])
        bytes_wait(r_in.at[c, pl.ds(1, PLANE - 1)], send_r.at[c])
    for cp in pair_copies:
        cp.wait_send()


def body(q, key_cache, value_cache, residual, norm_gain, ids, wts, w_gate, w_up, w_down):
    vmem = pl.BlockSpec(memory_space=pltpu.VMEM)
    hbm = pl.BlockSpec(memory_space=pl.ANY)
    dma = pltpu.SemaphoreType.DMA
    out = pl.pallas_call(
        kernel,
        out_shape=jax.ShapeDtypeStruct((2, D), BF),
        in_specs=[hbm] * 10,
        out_specs=vmem,
        scratch_shapes=[
            pltpu.SMEM((2, TOPK), jnp.int32),
            pltpu.SMEM((2, TOPK), F32),
            pltpu.VMEM((2, D), BF),
            pltpu.VMEM((2, D), BF),
            pltpu.VMEM((H, HD), F32),
            pltpu.VMEM((2, CTX, KVH * HD), BF),
            pltpu.VMEM((2, CTX, KVH * HD), BF),
            pltpu.VMEM((FF, D), BF),
            pltpu.VMEM((FF, D), BF),
            pltpu.VMEM((FF, D), BF),
            pltpu.VMEM((D, FF), BF),
            pltpu.VMEM((D, FF), BF),
            pltpu.VMEM((2 * H, HD), F32),
            pltpu.VMEM((2 * H, HD), F32),
            pltpu.VMEM((2, H, HD), F32),
            pltpu.VMEM((NC, 2 * HC, HD), BF),
            pltpu.VMEM((1, 128), F32),
            pltpu.VMEM((PLANE, 1, 128), F32),
            pltpu.VMEM((NC, PLANE, 2 * HC, HD), BF),
            pltpu.VMEM((2 * PLANE * HC, HD), F32),
            pltpu.VMEM((2 * PLANE, CW), BF),
            pltpu.VMEM((NC, 2 * NY, CAP, CW), BF),
            pltpu.VMEM((2 * NY * CAP, FF), F32),
            pltpu.VMEM((2 * NY * CAP, FF), F32),
            pltpu.VMEM((2 * NY * CAP, FF), BF),
            pltpu.VMEM((NC, 2 * NY, CAP, CW), BF),
            pltpu.VMEM((NC, NY, CAP, CW), BF),
            pltpu.VMEM((NC, NY, CAP, CW), BF),
            pltpu.VMEM((NC, NY - 1, CAP, CW), BF),
            pltpu.VMEM((NC, PLANE, 2 * HC, HD), BF),
            pltpu.VMEM((NC, PLANE, 2 * HC, HD), BF),
            dma((5,)),
            dma((4,)),
            dma((2 * NC + 1,)),
            dma((1,)),
            dma((1,)),
            dma((NC,)),
            dma((NC,)),
            dma((NC,)),
            dma((NC, NY)),
            dma((NC, NY)),
            dma((NC, NY)),
            dma((NC,)),
            dma((NC,)),
            dma((NC,)),
            dma((NC,)),
            dma((NC,)),
            dma((NC,)),
        ],
        compiler_params=pltpu.CompilerParams(
            collective_id=0, has_side_effects=True, vmem_limit_bytes=62 * 1024 * 1024
        ),
        cost_estimate=pl.CostEstimate(
            flops=6 * 128 * D * FF, bytes_accessed=3 * 2 * D * FF, transcendentals=128 * FF
        ),
        name="decode_layer",
    )(
        ids,
        wts,
        q,
        residual,
        norm_gain.reshape(H, HD),
        key_cache,
        value_cache,
        jnp.swapaxes(w_gate, 1, 2),
        jnp.swapaxes(w_up, 1, 2),
        w_down,
    )
    return out


def solution(mesh):
    return jax.shard_map(
        body,
        mesh=mesh,
        in_specs=(
            P(("dp", "expert"), None),
            P(("dp", "expert"), None, None),
            P(("dp", "expert"), None, None),
            P(("dp", "expert"), None),
            P(),
            P(("dp", "expert"), None),
            P(("dp", "expert"), None),
            P("expert", None, "dp"),
            P("expert", None, "dp"),
            P("expert", "dp", None),
        ),
        out_specs=P(("dp", "expert"), None),
        check_vma=False,
    )
```

```python
import jax
import jax.numpy as jnp
from jax import lax
from jax.experimental import pallas as pl
from jax.experimental.pallas import tpu as pltpu
from jax.sharding import PartitionSpec as P

MESH = pl.DeviceIdType.MESH
D = 6144
H = 48
KVH = 8
HD = 128
PER = H // KVH
TOPK = 4
CTX = 128
NY, NX, NZ = 4, 4, 4
PLANE = NX * NZ
CAP = 16
FF = 672
NC = 6
LAG = 3
DELAY = 6
EARLY = 4
FIRST = 4
HC = H // NC
CW = D // NC
BF = jnp.bfloat16
F32 = jnp.float32


def bytes_wait(ref, sem):
    pltpu.make_async_copy(ref, ref, sem).wait()


def across(a, b):
    return lax.dot_general(a, b, (((1,), (1,)), ((), ())), preferred_element_type=F32)


def total_of(a):
    return jnp.sum(jnp.sum(a, axis=0, keepdims=True), axis=1, keepdims=True)


def kernel(
    ids_hbm,
    wts_hbm,
    q_hbm,
    res_hbm,
    gain_hbm,
    key_hbm,
    val_hbm,
    gate_hbm,
    up_hbm,
    down_hbm,
    out_ref,
    ids_s,
    wts_s,
    q_ref,
    res_ref,
    gain_ref,
    key_v,
    val_v,
    gate_v,
    up_v,
    down_v,
    gate_t,
    up_t,
    rows_q,
    rows_res,
    hst,
    mine,
    mine_ids,
    ids_in,
    x_in,
    flat,
    x_t,
    x_all,
    acc_g,
    acc_u,
    act,
    part,
    pair_in,
    summed,
    y_in,
    joint,
    ret,
    r_in,
    sem_in,
    sem_kv,
    sem_w,
    send_i,
    recv_i,
    send_a,
    recv_a,
    send_y,
    recv_y,
    send_p,
    recv_p,
    send_q,
    recv_q,
    send_f,
    recv_f,
    send_j,
    recv_j,
    send_z,
    recv_z,
    send_r,
    recv_r,
):
    p = lax.axis_index("dp")
    e = lax.axis_index("expert")
    y, core = p // 2, lax.rem(p, 2)
    x, z = e // NZ, lax.rem(e, NZ)
    offsets = [(i, j) for i in range(NX) for j in range(NZ)]

    def plane_dev(i, j):
        return (p, lax.rem(x + i + NX, NX) * NZ + lax.rem(z + j + NZ, NZ))

    def y_dev(dy):
        return (lax.rem(y + dy + NY, NY) * 2 + core, e)

    pair = (y * 2 + 1 - core, e)
    side = 1 - 2 * core

    smalls = []
    for n, (src, dst) in enumerate(
        ((q_hbm, q_ref), (res_hbm, res_ref), (ids_hbm, ids_s), (wts_hbm, wts_s), (gain_hbm, gain_ref))
    ):
        cp = pltpu.make_async_copy(src, dst, sem_in.at[n])
        cp.start()
        smalls.append(cp)
    loads = []
    for r in range(2):
        for n, (src, dst) in enumerate(((key_hbm, key_v), (val_hbm, val_v))):
            cp = pltpu.make_async_copy(src.at[r], dst.at[r], sem_kv.at[2 * r + n])
            cp.start()
            loads.append(cp)

    barrier = pltpu.get_barrier_semaphore()
    greet = [plane_dev(i, j) for i, j in offsets[1:]] + [y_dev(d) for d in range(1, NY)] + [pair]
    for dev in greet:
        pl.semaphore_signal(barrier, inc=1, device_id=dev, device_id_type=MESH)

    smalls[0].wait()
    qf = q_ref[...].astype(F32)
    for h in range(H):
        rows_q[pl.ds(h, 2, stride=H), :] = qf[:, h * HD : (h + 1) * HD]
    head = lax.broadcasted_iota(jnp.int32, (H, HD), 0)
    masks = [(head >= PER * g) & (head < PER * (g + 1)) for g in range(KVH)]
    q_wide = []
    for r in range(2):
        q = rows_q[pl.ds(r * H, H), :]
        q_wide.append(
            jnp.concatenate([jnp.where(m, q, 0.0) for m in masks], axis=1).astype(BF)
        )
    smalls[1].wait()
    rf = res_ref[...].astype(F32)
    for h in range(H):
        rows_res[pl.ds(h, 2, stride=H), :] = rf[:, h * HD : (h + 1) * HD]
    for cp in smalls[2:]:
        cp.wait()

    lane = lax.broadcasted_iota(jnp.int32, (1, 128), 1)
    tile = jnp.zeros((1, 128), F32)
    for r in range(2):
        for k in range(TOPK):
            tile = jnp.where(lane == ids_s[r, k] + r * PLANE, 1.0, tile)
    mine_ids[...] = tile

    for cp in loads:
        cp.wait()
    w_loads = [
        pltpu.make_async_copy(
            src.at[0, :, pl.ds(c * CW, CW)], dst.at[:, pl.ds(c * CW, CW)], sem_w.at[2 * c + n]
        )
        for c in range(NC)
        for n, (src, dst) in enumerate(((gate_hbm, gate_v), (up_hbm, up_v)))
    ]
    w_loads.append(pltpu.make_async_copy(down_hbm.at[0], down_v, sem_w.at[2 * NC]))
    for cp in w_loads[: 2 * FIRST]:
        cp.start()

    def turn(c):
        for n, (src, dst) in enumerate(((gate_v, gate_t), (up_v, up_t))):
            w_loads[2 * c + n].wait()
            dst[c * CW : (c + 1) * CW, :] = jnp.transpose(src[:, c * CW : (c + 1) * CW])

    scores = jnp.concatenate([across(q_wide[r], key_v[r]) for r in range(2)], axis=0) * HD ** (-0.5)
    lifted = jnp.exp(scores - jnp.max(scores, axis=1, keepdims=True))
    probs = (lifted / jnp.sum(lifted, axis=1, keepdims=True)).astype(BF)
    gain = gain_ref[...]
    normed = []
    for r in range(2):
        wide = jnp.dot(probs[r * H : (r + 1) * H], val_v[r], preferred_element_type=F32)
        attended = jnp.zeros((H, HD), F32)
        for g in range(KVH):
            attended = jnp.where(masks[g], wide[:, g * HD : (g + 1) * HD], attended)
        hstate = (rows_res[pl.ds(r * H, H), :] + attended).astype(BF).astype(F32)
        hst[r] = hstate
        mean = total_of(hstate) * (1.0 / D)
        centered = hstate - mean
        var = total_of(centered * centered) * (1.0 / D)
        normed.append(centered * lax.rsqrt(var + 1e-05) * gain)
    for c in range(NC):
        block = jnp.concatenate([v[c * HC : (c + 1) * HC, :] for v in normed], axis=0).astype(BF)
        mine[c] = block
        x_in[c, 0] = block

    pl.semaphore_wait(barrier, len(greet))

    for n, (i, j) in enumerate(offsets):
        if n:
            pltpu.make_async_remote_copy(
                src_ref=mine_ids, dst_ref=ids_in.at[n], send_sem=send_i.at[0],
                recv_sem=recv_i.at[0], device_id=plane_dev(i, j), device_id_type=MESH,
            ).start()
    for c in range(NC):
        for n, (i, j) in enumerate(offsets):
            if n:
                pltpu.make_async_remote_copy(
                    src_ref=mine.at[c], dst_ref=x_in.at[c, n],
                    send_sem=send_a.at[c], recv_sem=recv_a.at[c],
                    device_id=plane_dev(i, j), device_id_type=MESH,
                ).start()
    for cp in w_loads[2 * FIRST :]:
        cp.start()
    for c in range(EARLY):
        turn(c)
    ids_in[0] = mine_ids[...]
    bytes_wait(ids_in.at[pl.ds(1, PLANE - 1)], recv_i.at[0])

    table = jnp.concatenate([ids_in[n] for n in range(PLANE)], axis=0)
    rowi = lax.broadcasted_iota(jnp.int32, (2 * PLANE, PLANE), 0)
    coli = lax.broadcasted_iota(jnp.int32, (2 * PLANE, PLANE), 1)
    twice = jnp.where(2 * coli == rowi - (rowi & 1), 1.0, 0.0)
    named = jnp.dot(twice, table, preferred_element_type=F32)
    mine_row = lax.broadcasted_iota(jnp.int32, (2 * PLANE, 128), 0)
    mine_lane = lax.broadcasted_iota(jnp.int32, (2 * PLANE, 128), 1)
    picked_c = jnp.sum(
        jnp.where(mine_lane == e + PLANE * (mine_row & 1), named, 0.0), axis=1, keepdims=True
    )
    picked_b = jnp.broadcast_to(picked_c, (2 * PLANE, 128))
    ri = lax.broadcasted_iota(jnp.int32, (2 * PLANE, 2 * PLANE), 0)
    ci = lax.broadcasted_iota(jnp.int32, (2 * PLANE, 2 * PLANE), 1)
    below = jnp.where(ci < ri, 1.0, 0.0)
    rank_b = jnp.dot(below, picked_b, preferred_element_type=F32)
    spread_f = jnp.where(
        (rank_b == mine_lane.astype(F32)) & (picked_b > 0.5), 1.0, 0.0
    )
    spread = spread_f[:, :CAP].astype(BF)
    ident = jnp.where(ri == ci, 1.0, 0.0)
    pick = lax.dot_general(
        spread_f, ident, (((0,), (0,)), ((), ())), preferred_element_type=F32
    )[:CAP, :].astype(BF)

    def forward(c, dy):
        cp = pltpu.make_async_remote_copy(
            src_ref=x_all.at[c, dy], dst_ref=x_all.at[c, NY + dy], send_sem=send_p.at[c, dy],
            recv_sem=recv_p.at[c, dy], device_id=pair, device_id_type=MESH,
        )
        cp.start()
        return cp

    pair_copies = []
    for c in range(NC):
        bytes_wait(x_in.at[c, pl.ds(1, PLANE - 1)], recv_a.at[c])
        flat[...] = x_in[c].astype(F32).reshape(2 * PLANE * HC, HD)
        for s in range(HC):
            x_t[:, s * HD : (s + 1) * HD] = flat[pl.ds(s, 2 * PLANE, stride=HC), :].astype(BF)
        x_all[c, 0] = jnp.dot(pick, x_t[...], preferred_element_type=F32).astype(BF)
        for dy in range(1, NY):
            pltpu.make_async_remote_copy(
                src_ref=x_all.at[c, 0], dst_ref=x_all.at[c, dy], send_sem=send_y.at[c],
                recv_sem=recv_y.at[c, dy], device_id=y_dev(dy), device_id_type=MESH,
            ).start()
        pair_copies.append(forward(c, 0))
        if c % 2 == 1 and EARLY + c // 2 < NC:
            turn(EARLY + c // 2)

    def forward_all(c):
        for dy in range(1, NY):
            bytes_wait(x_all.at[c, dy], recv_y.at[c, dy])
            pair_copies.append(forward(c, dy))

    def multiply(c):
        for dy in range(NY):
            bytes_wait(x_all.at[c, NY + dy], recv_p.at[c, dy])
        block = x_all[c].reshape(2 * NY * CAP, CW)
        gate = jnp.dot(block, gate_t[c * CW : (c + 1) * CW, :], preferred_element_type=F32)
        up = jnp.dot(block, up_t[c * CW : (c + 1) * CW, :], preferred_element_type=F32)
        if c < NC - 1:
            acc_g[...] = gate if c == 0 else acc_g[...] + gate
            acc_u[...] = up if c == 0 else acc_u[...] + up
        else:
            gate = acc_g[...] + gate
            up = acc_u[...] + up
            act[...] = (gate / (1.0 + jnp.exp(-gate)) * up).astype(BF)

    forward_all(0)
    for c in range(NC):
        if c < NC - 1:
            forward_all(c + 1)
        multiply(c)

    w_loads[2 * NC].wait()

    def down(n):
        out = jnp.dot(
            act[...], down_v[:, n * CW : (n + 1) * CW], preferred_element_type=F32
        ).astype(BF)
        part[n] = out.reshape(2 * NY, CAP, CW)
        pltpu.make_async_remote_copy(
            src_ref=part.at[n, pl.ds(NY, NY)], dst_ref=pair_in.at[n], send_sem=send_q.at[n],
            recv_sem=recv_q.at[n], device_id=pair, device_id_type=MESH,
        ).start()

    def pair_sum(n):
        bytes_wait(pair_in.at[n], recv_q.at[n])
        summed[n] = (part[n, :NY].astype(F32) + pair_in[n].astype(F32)).astype(BF)
        pltpu.make_async_remote_copy(
            src_ref=summed.at[n, 2], dst_ref=y_in.at[n, 2], send_sem=send_f.at[n],
            recv_sem=recv_f.at[n], device_id=y_dev(side), device_id_type=MESH,
        ).start()

    def direct(n):
        pltpu.make_async_remote_copy(
            src_ref=summed.at[n, 1 + 2 * core], dst_ref=y_in.at[n, 0], send_sem=send_z.at[n],
            recv_sem=recv_z.at[n], device_id=y_dev(-side), device_id_type=MESH,
        ).start()

    def combine(n):
        bytes_wait(y_in.at[n, 2], recv_f.at[n])
        joint[n] = (summed[n, 3 - 2 * core].astype(F32) + y_in[n, 2].astype(F32)).astype(BF)
        pltpu.make_async_remote_copy(
            src_ref=joint.at[n], dst_ref=y_in.at[n, 1], send_sem=send_j.at[n],
            recv_sem=recv_j.at[n], device_id=y_dev(side), device_id_type=MESH,
        ).start()

    for n in range(NC):
        down(n)
        if n >= LAG:
            pair_sum(n - LAG)
            if n - LAG >= DELAY:
                direct(n - LAG - DELAY)
    for n in range(NC - LAG, NC):
        pair_sum(n)
        if n >= DELAY:
            direct(n - DELAY)
    for n in range(NC - DELAY, NC):
        direct(n)
    for n in range(NC):
        combine(n)

    for n in range(NC):
        bytes_wait(y_in.at[n, 0], recv_z.at[n])
        bytes_wait(y_in.at[n, 1], recv_j.at[n])
        total = summed[n, 0].astype(F32) + y_in[n, 0].astype(F32) + y_in[n, 1].astype(F32)
        back = jnp.dot(spread, total.astype(BF), preferred_element_type=F32)
        for s in range(HC):
            flat[pl.ds(s, 2 * PLANE, stride=HC), :] = back[:, s * HD : (s + 1) * HD]
        ret[n] = flat[...].astype(BF).reshape(PLANE, 2 * HC, HD)
        for m, (i, j) in enumerate(offsets):
            if m:
                pltpu.make_async_remote_copy(
                    src_ref=ret.at[n, m], dst_ref=r_in.at[n, m], send_sem=send_r.at[n],
                    recv_sem=recv_r.at[n], device_id=plane_dev(-i, -j), device_id_type=MESH,
                ).start()

    weights = []
    for r in range(2):
        row = []
        for i, j in offsets:
            expert = plane_dev(i, j)[1]
            w = jnp.float32(0.0)
            for k in range(TOPK):
                w = w + jnp.where(ids_s[r, k] == expert, wts_s[r, k], 0.0)
            row.append(w)
        weights.append(row)
    for n in range(NC):
        bytes_wait(r_in.at[n, pl.ds(1, PLANE - 1)], recv_r.at[n])
        replies = [ret[n, 0].astype(F32)] + [r_in[n, m].astype(F32) for m in range(1, PLANE)]
        for r in range(2):
            total = hst[r, n * HC : (n + 1) * HC, :]
            for m in range(PLANE):
                got = replies[m][r * HC : (r + 1) * HC, :]
                total = total + weights[r][m] * got
            rows_q[pl.ds(r * H + n * HC, HC), :] = total
    for h in range(H):
        out_ref[:, h * HD : (h + 1) * HD] = rows_q[pl.ds(h, 2, stride=H), :].astype(BF)

    bytes_wait(ids_in.at[pl.ds(1, PLANE - 1)], send_i.at[0])
    for c in range(NC):
        bytes_wait(x_in.at[c, pl.ds(1, PLANE - 1)], send_a.at[c])
        bytes_wait(x_all.at[c, pl.ds(1, NY - 1)], send_y.at[c])
        bytes_wait(pair_in.at[c], send_q.at[c])
        bytes_wait(y_in.at[c, 0], send_z.at[c])
        bytes_wait(y_in.at[c, 2], send_f.at[c])
        bytes_wait(joint.at[c], send_j.at[c])
        bytes_wait(r_in.at[c, pl.ds(1, PLANE - 1)], send_r.at[c])
    for cp in pair_copies:
        cp.wait_send()


def body(q, key_cache, value_cache, residual, norm_gain, ids, wts, w_gate, w_up, w_down):
    vmem = pl.BlockSpec(memory_space=pltpu.VMEM)
    hbm = pl.BlockSpec(memory_space=pl.ANY)
    dma = pltpu.SemaphoreType.DMA
    out = pl.pallas_call(
        kernel,
        out_shape=jax.ShapeDtypeStruct((2, D), BF),
        in_specs=[hbm] * 10,
        out_specs=vmem,
        scratch_shapes=[
            pltpu.SMEM((2, TOPK), jnp.int32),
            pltpu.SMEM((2, TOPK), F32),
            pltpu.VMEM((2, D), BF),
            pltpu.VMEM((2, D), BF),
            pltpu.VMEM((H, HD), F32),
            pltpu.VMEM((2, CTX, KVH * HD), BF),
            pltpu.VMEM((2, CTX, KVH * HD), BF),
            pltpu.VMEM((FF, D), BF),
            pltpu.VMEM((FF, D), BF),
            pltpu.VMEM((FF, D), BF),
            pltpu.VMEM((D, FF), BF),
            pltpu.VMEM((D, FF), BF),
            pltpu.VMEM((2 * H, HD), F32),
            pltpu.VMEM((2 * H, HD), F32),
            pltpu.VMEM((2, H, HD), F32),
            pltpu.VMEM((NC, 2 * HC, HD), BF),
            pltpu.VMEM((1, 128), F32),
            pltpu.VMEM((PLANE, 1, 128), F32),
            pltpu.VMEM((NC, PLANE, 2 * HC, HD), BF),
            pltpu.VMEM((2 * PLANE * HC, HD), F32),
            pltpu.VMEM((2 * PLANE, CW), BF),
            pltpu.VMEM((NC, 2 * NY, CAP, CW), BF),
            pltpu.VMEM((2 * NY * CAP, FF), F32),
            pltpu.VMEM((2 * NY * CAP, FF), F32),
            pltpu.VMEM((2 * NY * CAP, FF), BF),
            pltpu.VMEM((NC, 2 * NY, CAP, CW), BF),
            pltpu.VMEM((NC, NY, CAP, CW), BF),
            pltpu.VMEM((NC, NY, CAP, CW), BF),
            pltpu.VMEM((NC, NY - 1, CAP, CW), BF),
            pltpu.VMEM((NC, CAP, CW), BF),
            pltpu.VMEM((NC, PLANE, 2 * HC, HD), BF),
            pltpu.VMEM((NC, PLANE, 2 * HC, HD), BF),
            dma((5,)),
            dma((4,)),
            dma((2 * NC + 1,)),
            dma((1,)),
            dma((1,)),
            dma((NC,)),
            dma((NC,)),
            dma((NC,)),
            dma((NC, NY)),
            dma((NC, NY)),
            dma((NC, NY)),
            dma((NC,)),
            dma((NC,)),
            dma((NC,)),
            dma((NC,)),
            dma((NC,)),
            dma((NC,)),
            dma((NC,)),
            dma((NC,)),
            dma((NC,)),
            dma((NC,)),
        ],
        compiler_params=pltpu.CompilerParams(
            collective_id=0, has_side_effects=True, vmem_limit_bytes=62 * 1024 * 1024
        ),
        cost_estimate=pl.CostEstimate(
            flops=6 * 128 * D * FF, bytes_accessed=3 * 2 * D * FF, transcendentals=128 * FF
        ),
        name="decode_layer",
    )(
        ids,
        wts,
        q,
        residual,
        norm_gain.reshape(H, HD),
        key_cache,
        value_cache,
        jnp.swapaxes(w_gate, 1, 2),
        jnp.swapaxes(w_up, 1, 2),
        w_down,
    )
    return out


def solution(mesh):
    return jax.shard_map(
        body,
        mesh=mesh,
        in_specs=(
            P(("dp", "expert"), None),
            P(("dp", "expert"), None, None),
            P(("dp", "expert"), None, None),
            P(("dp", "expert"), None),
            P(),
            P(("dp", "expert"), None),
            P(("dp", "expert"), None),
            P("expert", None, "dp"),
            P("expert", None, "dp"),
            P("expert", "dp", None),
        ),
        out_specs=P(("dp", "expert"), None),
        check_vma=False,
    )
```

```python
import jax
import jax.numpy as jnp
from jax import lax
from jax.experimental import pallas as pl
from jax.experimental.pallas import tpu as pltpu
from jax.sharding import PartitionSpec as P

MESH = pl.DeviceIdType.MESH
D = 6144
H = 48
KVH = 8
HD = 128
PER = H // KVH
TOPK = 4
CTX = 128
NY, NX, NZ = 4, 4, 4
PLANE = NX * NZ
CAP = 16
FF = 672
NC = 6
LAG = 3
DELAY = 6
EARLY = 4
FIRST = 4
HC = H // NC
CW = D // NC
BF = jnp.bfloat16
F32 = jnp.float32


def bytes_wait(ref, sem):
    pltpu.make_async_copy(ref, ref, sem).wait()


def across(a, b):
    return lax.dot_general(a, b, (((1,), (1,)), ((), ())), preferred_element_type=F32)


def total_of(a):
    return jnp.sum(jnp.sum(a, axis=0, keepdims=True), axis=1, keepdims=True)


def kernel(
    ids_hbm,
    wts_hbm,
    q_hbm,
    res_hbm,
    gain_hbm,
    key_hbm,
    val_hbm,
    gate_hbm,
    up_hbm,
    down_hbm,
    out_ref,
    ids_s,
    wts_s,
    q_ref,
    res_ref,
    gain_ref,
    key_v,
    val_v,
    gate_v,
    up_v,
    down_v,
    gate_t,
    up_t,
    rows_q,
    rows_res,
    hst,
    mine,
    mine_ids,
    ids_in,
    x_in,
    flat,
    x_t,
    x_all,
    acc_g,
    acc_u,
    act,
    part,
    pair_in,
    summed,
    y_in,
    joint,
    ret,
    r_in,
    sem_in,
    sem_kv,
    sem_w,
    send_i,
    recv_i,
    send_a,
    recv_a,
    send_y,
    recv_y,
    send_p,
    recv_p,
    send_q,
    recv_q,
    send_f,
    recv_f,
    send_j,
    recv_j,
    send_z,
    recv_z,
    send_r,
    recv_r,
):
    p = lax.axis_index("dp")
    e = lax.axis_index("expert")
    y, core = p // 2, lax.rem(p, 2)
    x, z = e // NZ, lax.rem(e, NZ)
    offsets = [(i, j) for i in range(NX) for j in range(NZ)]

    def plane_dev(i, j):
        return (p, lax.rem(x + i + NX, NX) * NZ + lax.rem(z + j + NZ, NZ))

    def y_dev(dy):
        return (lax.rem(y + dy + NY, NY) * 2 + core, e)

    pair = (y * 2 + 1 - core, e)
    side = 1 - 2 * core

    smalls = []
    for n, (src, dst) in enumerate(
        ((q_hbm, q_ref), (res_hbm, res_ref), (ids_hbm, ids_s), (wts_hbm, wts_s), (gain_hbm, gain_ref))
    ):
        cp = pltpu.make_async_copy(src, dst, sem_in.at[n])
        cp.start()
        smalls.append(cp)
    loads = []
    for r, n in ((0, 0), (1, 0), (0, 1), (1, 1)):
        src, dst = ((key_hbm, key_v), (val_hbm, val_v))[n]
        cp = pltpu.make_async_copy(src.at[r], dst.at[r], sem_kv.at[2 * r + n])
        cp.start()
        loads.append(cp)

    barrier = pltpu.get_barrier_semaphore()
    greet = [plane_dev(i, j) for i, j in offsets[1:]] + [y_dev(d) for d in range(1, NY)] + [pair]
    for dev in greet:
        pl.semaphore_signal(barrier, inc=1, device_id=dev, device_id_type=MESH)

    smalls[0].wait()
    qf = q_ref[...].astype(F32)
    for h in range(H):
        rows_q[pl.ds(h, 2, stride=H), :] = qf[:, h * HD : (h + 1) * HD]
    head = lax.broadcasted_iota(jnp.int32, (H, HD), 0)
    masks = [(head >= PER * g) & (head < PER * (g + 1)) for g in range(KVH)]
    q_wide = []
    for r in range(2):
        q = rows_q[pl.ds(r * H, H), :]
        q_wide.append(
            jnp.concatenate([jnp.where(m, q, 0.0) for m in masks], axis=1).astype(BF)
        )
    smalls[1].wait()
    rf = res_ref[...].astype(F32)
    for h in range(H):
        rows_res[pl.ds(h, 2, stride=H), :] = rf[:, h * HD : (h + 1) * HD]
    for cp in smalls[2:]:
        cp.wait()

    lane = lax.broadcasted_iota(jnp.int32, (1, 128), 1)
    tile = jnp.zeros((1, 128), F32)
    for r in range(2):
        for k in range(TOPK):
            tile = jnp.where(lane == ids_s[r, k] + r * PLANE, 1.0, tile)
    mine_ids[...] = tile

    for cp in loads[:2]:
        cp.wait()
    scores = jnp.concatenate([across(q_wide[r], key_v[r]) for r in range(2)], axis=0) * HD ** (-0.5)
    for cp in loads[2:]:
        cp.wait()
    w_loads = [
        pltpu.make_async_copy(
            src.at[0, :, pl.ds(c * CW, CW)], dst.at[:, pl.ds(c * CW, CW)], sem_w.at[2 * c + n]
        )
        for c in range(NC)
        for n, (src, dst) in enumerate(((gate_hbm, gate_v), (up_hbm, up_v)))
    ]
    w_loads.append(pltpu.make_async_copy(down_hbm.at[0], down_v, sem_w.at[2 * NC]))
    for cp in w_loads[: 2 * FIRST]:
        cp.start()

    def turn(c):
        for n, (src, dst) in enumerate(((gate_v, gate_t), (up_v, up_t))):
            w_loads[2 * c + n].wait()
            dst[c * CW : (c + 1) * CW, :] = jnp.transpose(src[:, c * CW : (c + 1) * CW])

    lifted = jnp.exp(scores - jnp.max(scores, axis=1, keepdims=True))
    probs = (lifted / jnp.sum(lifted, axis=1, keepdims=True)).astype(BF)
    gain = gain_ref[...]
    normed = []
    for r in range(2):
        wide = jnp.dot(probs[r * H : (r + 1) * H], val_v[r], preferred_element_type=F32)
        attended = jnp.zeros((H, HD), F32)
        for g in range(KVH):
            attended = jnp.where(masks[g], wide[:, g * HD : (g + 1) * HD], attended)
        hstate = (rows_res[pl.ds(r * H, H), :] + attended).astype(BF).astype(F32)
        hst[r] = hstate
        mean = total_of(hstate) * (1.0 / D)
        centered = hstate - mean
        var = total_of(centered * centered) * (1.0 / D)
        normed.append(centered * lax.rsqrt(var + 1e-05) * gain)
    for c in range(NC):
        block = jnp.concatenate([v[c * HC : (c + 1) * HC, :] for v in normed], axis=0).astype(BF)
        mine[c] = block
        x_in[c, 0] = block

    pl.semaphore_wait(barrier, len(greet))

    for n, (i, j) in enumerate(offsets):
        if n:
            pltpu.make_async_remote_copy(
                src_ref=mine_ids, dst_ref=ids_in.at[n], send_sem=send_i.at[0],
                recv_sem=recv_i.at[0], device_id=plane_dev(i, j), device_id_type=MESH,
            ).start()
    for c in range(NC):
        for n, (i, j) in enumerate(offsets):
            if n:
                pltpu.make_async_remote_copy(
                    src_ref=mine.at[c], dst_ref=x_in.at[c, n],
                    send_sem=send_a.at[c], recv_sem=recv_a.at[c],
                    device_id=plane_dev(i, j), device_id_type=MESH,
                ).start()
    for cp in w_loads[2 * FIRST :]:
        cp.start()
    for c in range(EARLY):
        turn(c)
    ids_in[0] = mine_ids[...]
    bytes_wait(ids_in.at[pl.ds(1, PLANE - 1)], recv_i.at[0])

    table = jnp.concatenate([ids_in[n] for n in range(PLANE)], axis=0)
    rowi = lax.broadcasted_iota(jnp.int32, (2 * PLANE, PLANE), 0)
    coli = lax.broadcasted_iota(jnp.int32, (2 * PLANE, PLANE), 1)
    twice = jnp.where(2 * coli == rowi - (rowi & 1), 1.0, 0.0)
    named = jnp.dot(twice, table, preferred_element_type=F32)
    mine_row = lax.broadcasted_iota(jnp.int32, (2 * PLANE, 128), 0)
    mine_lane = lax.broadcasted_iota(jnp.int32, (2 * PLANE, 128), 1)
    picked_c = jnp.sum(
        jnp.where(mine_lane == e + PLANE * (mine_row & 1), named, 0.0), axis=1, keepdims=True
    )
    picked_b = jnp.broadcast_to(picked_c, (2 * PLANE, 128))
    ri = lax.broadcasted_iota(jnp.int32, (2 * PLANE, 2 * PLANE), 0)
    ci = lax.broadcasted_iota(jnp.int32, (2 * PLANE, 2 * PLANE), 1)
    below = jnp.where(ci < ri, 1.0, 0.0)
    rank_b = jnp.dot(below, picked_b, preferred_element_type=F32)
    spread_f = jnp.where(
        (rank_b == mine_lane.astype(F32)) & (picked_b > 0.5), 1.0, 0.0
    )
    spread = spread_f[:, :CAP].astype(BF)
    ident = jnp.where(ri == ci, 1.0, 0.0)
    pick = lax.dot_general(
        spread_f, ident, (((0,), (0,)), ((), ())), preferred_element_type=F32
    )[:CAP, :].astype(BF)

    def forward(c, first, count):
        cp = pltpu.make_async_remote_copy(
            src_ref=x_all.at[c, pl.ds(first, count)],
            dst_ref=x_all.at[c, pl.ds(NY + first, count)],
            send_sem=send_p.at[c, min(first, 1)], recv_sem=recv_p.at[c],
            device_id=pair, device_id_type=MESH,
        )
        cp.start()
        return cp

    pair_copies = []
    for c in range(NC):
        bytes_wait(x_in.at[c, pl.ds(1, PLANE - 1)], recv_a.at[c])
        flat[...] = x_in[c].astype(F32).reshape(2 * PLANE * HC, HD)
        for s in range(HC):
            x_t[:, s * HD : (s + 1) * HD] = flat[pl.ds(s, 2 * PLANE, stride=HC), :].astype(BF)
        x_all[c, 0] = jnp.dot(pick, x_t[...], preferred_element_type=F32).astype(BF)
        for dy in range(1, NY):
            pltpu.make_async_remote_copy(
                src_ref=x_all.at[c, 0], dst_ref=x_all.at[c, dy], send_sem=send_y.at[c],
                recv_sem=recv_y.at[c], device_id=y_dev(dy), device_id_type=MESH,
            ).start()
        pair_copies.append(forward(c, 0, 1))
        if c % 2 == 1 and EARLY + c // 2 < NC:
            turn(EARLY + c // 2)

    def forward_all(c):
        bytes_wait(x_all.at[c, pl.ds(1, NY - 1)], recv_y.at[c])
        pair_copies.append(forward(c, 1, NY - 1))

    def multiply(c):
        bytes_wait(x_all.at[c, pl.ds(NY, NY)], recv_p.at[c])
        block = x_all[c].reshape(2 * NY * CAP, CW)
        gate = jnp.dot(block, gate_t[c * CW : (c + 1) * CW, :], preferred_element_type=F32)
        up = jnp.dot(block, up_t[c * CW : (c + 1) * CW, :], preferred_element_type=F32)
        if c < NC - 1:
            acc_g[...] = gate if c == 0 else acc_g[...] + gate
            acc_u[...] = up if c == 0 else acc_u[...] + up
        else:
            gate = acc_g[...] + gate
            up = acc_u[...] + up
            act[...] = (gate / (1.0 + jnp.exp(-gate)) * up).astype(BF)

    forward_all(0)
    for c in range(NC):
        if c < NC - 1:
            forward_all(c + 1)
        multiply(c)

    w_loads[2 * NC].wait()

    def down(n):
        out = jnp.dot(
            act[...], down_v[:, n * CW : (n + 1) * CW], preferred_element_type=F32
        ).astype(BF)
        part[n] = out.reshape(2 * NY, CAP, CW)
        pltpu.make_async_remote_copy(
            src_ref=part.at[n, pl.ds(NY, NY)], dst_ref=pair_in.at[n], send_sem=send_q.at[n],
            recv_sem=recv_q.at[n], device_id=pair, device_id_type=MESH,
        ).start()

    def pair_sum(n):
        bytes_wait(pair_in.at[n], recv_q.at[n])
        summed[n] = (part[n, :NY].astype(F32) + pair_in[n].astype(F32)).astype(BF)
        pltpu.make_async_remote_copy(
            src_ref=summed.at[n, 2], dst_ref=y_in.at[n, 2], send_sem=send_f.at[n],
            recv_sem=recv_f.at[n], device_id=y_dev(side), device_id_type=MESH,
        ).start()

    def direct(n):
        pltpu.make_async_remote_copy(
            src_ref=summed.at[n, 1 + 2 * core], dst_ref=y_in.at[n, 0], send_sem=send_z.at[n],
            recv_sem=recv_z.at[n], device_id=y_dev(-side), device_id_type=MESH,
        ).start()

    def combine(n):
        bytes_wait(y_in.at[n, 2], recv_f.at[n])
        joint[n] = (summed[n, 3 - 2 * core].astype(F32) + y_in[n, 2].astype(F32)).astype(BF)
        pltpu.make_async_remote_copy(
            src_ref=joint.at[n], dst_ref=y_in.at[n, 1], send_sem=send_j.at[n],
            recv_sem=recv_j.at[n], device_id=y_dev(side), device_id_type=MESH,
        ).start()

    for n in range(NC):
        down(n)
        if n >= LAG:
            pair_sum(n - LAG)
            if n - LAG >= DELAY:
                direct(n - LAG - DELAY)
    for n in range(NC - LAG, NC):
        pair_sum(n)
        if n >= DELAY:
            direct(n - DELAY)
    for n in range(NC - DELAY, NC):
        direct(n)
    for n in range(NC):
        combine(n)

    for n in range(NC):
        bytes_wait(y_in.at[n, 0], recv_z.at[n])
        bytes_wait(y_in.at[n, 1], recv_j.at[n])
        total = summed[n, 0].astype(F32) + y_in[n, 0].astype(F32) + y_in[n, 1].astype(F32)
        back = jnp.dot(spread, total.astype(BF), preferred_element_type=F32)
        for s in range(HC):
            flat[pl.ds(s, 2 * PLANE, stride=HC), :] = back[:, s * HD : (s + 1) * HD]
        ret[n] = flat[...].astype(BF).reshape(PLANE, 2 * HC, HD)
        for m, (i, j) in enumerate(offsets):
            if m:
                pltpu.make_async_remote_copy(
                    src_ref=ret.at[n, m], dst_ref=r_in.at[n, m], send_sem=send_r.at[n],
                    recv_sem=recv_r.at[n], device_id=plane_dev(-i, -j), device_id_type=MESH,
                ).start()

    weights = []
    for r in range(2):
        row = []
        for i, j in offsets:
            expert = plane_dev(i, j)[1]
            w = jnp.float32(0.0)
            for k in range(TOPK):
                w = w + jnp.where(ids_s[r, k] == expert, wts_s[r, k], 0.0)
            row.append(w)
        weights.append(row)
    for n in range(NC):
        bytes_wait(r_in.at[n, pl.ds(1, PLANE - 1)], recv_r.at[n])
        replies = [ret[n, 0].astype(F32)] + [r_in[n, m].astype(F32) for m in range(1, PLANE)]
        for r in range(2):
            total = hst[r, n * HC : (n + 1) * HC, :]
            for m in range(PLANE):
                got = replies[m][r * HC : (r + 1) * HC, :]
                total = total + weights[r][m] * got
            rows_q[pl.ds(r * H + n * HC, HC), :] = total
    for h in range(H):
        out_ref[:, h * HD : (h + 1) * HD] = rows_q[pl.ds(h, 2, stride=H), :].astype(BF)

    bytes_wait(ids_in.at[pl.ds(1, PLANE - 1)], send_i.at[0])
    for c in range(NC):
        bytes_wait(x_in.at[c, pl.ds(1, PLANE - 1)], send_a.at[c])
        bytes_wait(x_all.at[c, pl.ds(1, NY - 1)], send_y.at[c])
        bytes_wait(pair_in.at[c], send_q.at[c])
        bytes_wait(y_in.at[c, 0], send_z.at[c])
        bytes_wait(y_in.at[c, 2], send_f.at[c])
        bytes_wait(joint.at[c], send_j.at[c])
        bytes_wait(r_in.at[c, pl.ds(1, PLANE - 1)], send_r.at[c])
    for cp in pair_copies:
        cp.wait_send()


def body(q, key_cache, value_cache, residual, norm_gain, ids, wts, w_gate, w_up, w_down):
    vmem = pl.BlockSpec(memory_space=pltpu.VMEM)
    hbm = pl.BlockSpec(memory_space=pl.ANY)
    dma = pltpu.SemaphoreType.DMA
    out = pl.pallas_call(
        kernel,
        out_shape=jax.ShapeDtypeStruct((2, D), BF),
        in_specs=[hbm] * 10,
        out_specs=vmem,
        scratch_shapes=[
            pltpu.SMEM((2, TOPK), jnp.int32),
            pltpu.SMEM((2, TOPK), F32),
            pltpu.VMEM((2, D), BF),
            pltpu.VMEM((2, D), BF),
            pltpu.VMEM((H, HD), F32),
            pltpu.VMEM((2, CTX, KVH * HD), BF),
            pltpu.VMEM((2, CTX, KVH * HD), BF),
            pltpu.VMEM((FF, D), BF),
            pltpu.VMEM((FF, D), BF),
            pltpu.VMEM((FF, D), BF),
            pltpu.VMEM((D, FF), BF),
            pltpu.VMEM((D, FF), BF),
            pltpu.VMEM((2 * H, HD), F32),
            pltpu.VMEM((2 * H, HD), F32),
            pltpu.VMEM((2, H, HD), F32),
            pltpu.VMEM((NC, 2 * HC, HD), BF),
            pltpu.VMEM((1, 128), F32),
            pltpu.VMEM((PLANE, 1, 128), F32),
            pltpu.VMEM((NC, PLANE, 2 * HC, HD), BF),
            pltpu.VMEM((2 * PLANE * HC, HD), F32),
            pltpu.VMEM((2 * PLANE, CW), BF),
            pltpu.VMEM((NC, 2 * NY, CAP, CW), BF),
            pltpu.VMEM((2 * NY * CAP, FF), F32),
            pltpu.VMEM((2 * NY * CAP, FF), F32),
            pltpu.VMEM((2 * NY * CAP, FF), BF),
            pltpu.VMEM((NC, 2 * NY, CAP, CW), BF),
            pltpu.VMEM((NC, NY, CAP, CW), BF),
            pltpu.VMEM((NC, NY, CAP, CW), BF),
            pltpu.VMEM((NC, NY - 1, CAP, CW), BF),
            pltpu.VMEM((NC, CAP, CW), BF),
            pltpu.VMEM((NC, PLANE, 2 * HC, HD), BF),
            pltpu.VMEM((NC, PLANE, 2 * HC, HD), BF),
            dma((5,)),
            dma((4,)),
            dma((2 * NC + 1,)),
            dma((1,)),
            dma((1,)),
            dma((NC,)),
            dma((NC,)),
            dma((NC,)),
            dma((NC,)),
            dma((NC, 2)),
            dma((NC,)),
            dma((NC,)),
            dma((NC,)),
            dma((NC,)),
            dma((NC,)),
            dma((NC,)),
            dma((NC,)),
            dma((NC,)),
            dma((NC,)),
            dma((NC,)),
            dma((NC,)),
        ],
        compiler_params=pltpu.CompilerParams(
            collective_id=0, has_side_effects=True, vmem_limit_bytes=62 * 1024 * 1024
        ),
        cost_estimate=pl.CostEstimate(
            flops=6 * 128 * D * FF, bytes_accessed=3 * 2 * D * FF, transcendentals=128 * FF
        ),
        name="decode_layer",
    )(
        ids,
        wts,
        q,
        residual,
        norm_gain.reshape(H, HD),
        key_cache,
        value_cache,
        jnp.swapaxes(w_gate, 1, 2),
        jnp.swapaxes(w_up, 1, 2),
        w_down,
    )
    return out


def solution(mesh):
    return jax.shard_map(
        body,
        mesh=mesh,
        in_specs=(
            P(("dp", "expert"), None),
            P(("dp", "expert"), None, None),
            P(("dp", "expert"), None, None),
            P(("dp", "expert"), None),
            P(),
            P(("dp", "expert"), None),
            P(("dp", "expert"), None),
            P("expert", None, "dp"),
            P("expert", None, "dp"),
            P("expert", "dp", None),
        ),
        out_specs=P(("dp", "expert"), None),
        check_vma=False,
    )
```
